32 devices in a mesh: groups: 2 (over x), seqt: 16 (over z, y, core).
Axes of the slice: x: 2, y: 2, z: 4, core: 2. Of those that a mesh axis runs over, the one named last changes fastest.
Arguments:
- out_grad: bfloat16 [4096, 4096], P(('groups', 'seqt')), parts along dimension 0, may hold values from -6 to 6
- hidden: bfloat16 [4096, 16384], P(('groups', 'seqt')), parts along dimension 0, may hold values from -0.13183594 to 0.13183594
- down_tiles: bfloat16 [128, 4, 128, 128], P('seqt'), may hold values from -0.3125 to 0.3125
- row_blocks: int32 [16, 4], replicated, may hold values from 0 to 31, as said below
- tile_mask: int32 [128, 4], P('seqt'), may hold values 0 or 1
Outputs:
- grad_hidden: bfloat16 [4096, 16384], P(('groups', 'seqt')), parts along dimension 0
- grad_tiles: float32 [256, 4, 128, 128], P(('groups', 'seqt')), parts along dimension 0
The draws below stay inside these ranges and needn't reach their ends.
There are 2 independent parts, one for each index of `groups`. The reference program is written for one: setup_inputs(seed, part) draws one part's arguments, and reference() takes and returns one part's arrays. A program takes and returns all parts, laid end to end along the dimension named above; an argument that names none is the same for every part. Nothing has to cross between parts.
Inputs may be any that keep to these rules, and one draw needn't show every extreme that they name: `row_blocks`: the 4 row blocks of one device are distinct.
All inputs are finite; a program needn't handle non-finite values. No bound on the sum of `tile_mask` on one device may be relied on, other than what follows from the above.
Results may differ from the reference program's by a relative error of at most 0.001.
Values may be sent and summed in bfloat16 or wider, within the bound.
A program may use at most 128 MiB of HBM per device.

```python
import jax
import jax.numpy as jnp
from jax import lax

D = 4096
FF = 16384
TILE = 128
RSET = 4
TOK_DEV = 128
TOKENS = 2048
RT = 32
CT = 128
N_SEQT = 16


def draw_row_blocks(key, part):
    subkeys = jax.random.split(key, N_SEQT)

    def device_rows(subkey):
        return jax.random.permutation(subkey, RT)[:RSET]
    return jax.vmap(device_rows)(subkeys).astype(jnp.int32)


def with_ends(values, stream_key, low, top_value):
    dims = values.shape
    spot = [jax.random.randint(jax.random.fold_in(stream_key, axis), (), 0, dims[axis]) for axis in range(len(dims))]
    values = values.at[tuple(spot)].set(low)
    longest = dims.index(max(dims))
    spot[longest] = (spot[longest] + 1) % dims[longest]
    return values.at[tuple(spot)].set(top_value)


def block_scale(rng, dims, cuts, smallest, largest):
    factor_of, own = 1.0, jax.random.fold_in(rng, 6)
    for position, parts in cuts:
        steps = jnp.exp(jax.random.uniform(jax.random.fold_in(own, position), (parts,), jnp.float32, smallest / len(cuts), largest / len(cuts)))
        factor_of = factor_of * jnp.repeat(steps, dims[position] // parts).reshape([-1 if axis == position else 1 for axis in range(len(dims))])
    return factor_of


def noise(key, shape, width, limit, pieces=(), kind=jnp.bfloat16):
    values = jax.random.normal(key, shape, jnp.float32) * width
    if len(pieces) > 0:
        values = block_scale(key, shape, pieces, -0.22, 0.18) * values
    return jnp.clip(values, min=-limit, max=limit).astype(kind)


def setup_inputs(seed: int = 0, part: int = 0) -> dict:
    arg_keys = jax.random.split(jax.random.key(seed), 6)
    own_keys = jax.random.split(jax.random.fold_in(arg_keys[5], part), 6)
    return {
        "out_grad": noise(own_keys[0], (TOKENS, D), 1.0, 6.0, ((0, 16),)),
        "hidden": noise(own_keys[1], (TOKENS, FF), ((TOK_DEV * N_SEQT) ** -0.5), 0.13183594, ((0, 16),)),
        "down_tiles": noise(arg_keys[2], (CT, RSET, TILE, TILE), (RSET * TILE * 4 // 5) ** -0.5, 0.3125, ((0, 16),)),
        "row_blocks": draw_row_blocks(jax.random.fold_in(arg_keys[5], 71), part),
        "tile_mask": with_ends((jax.random.randint(arg_keys[4], (CT, RSET), 0, 5) < 4).astype(jnp.int32), jax.random.fold_in(arg_keys[4], 1), 0, 1),
    }


def reference(out_grad, hidden, down_tiles, row_blocks, tile_mask):
    token_count = out_grad.shape[0]
    col_count = FF // (TILE * N_SEQT)
    grad_blocks = out_grad.reshape(token_count, D // TILE, TILE)
    tiles_dev = down_tiles.reshape(N_SEQT, col_count, RSET, TILE, TILE)
    masks_dev = tile_mask.reshape(N_SEQT, col_count, RSET)

    def per_device(device):
        row_list = lax.dynamic_index_in_dim(row_blocks, device, 0, keepdims=False)
        picked = jnp.take(grad_blocks, row_list, axis=1).reshape(token_count, RSET * TILE)
        tile_set = lax.dynamic_index_in_dim(tiles_dev, device, 0, keepdims=False)
        mask_set = lax.dynamic_index_in_dim(masks_dev, device, 0, keepdims=False)
        masked = tile_set * mask_set[:, :, None, None].astype(tile_set.dtype)
        weight_mat = masked.transpose(0, 2, 1, 3).reshape(col_count * TILE, RSET * TILE)
        grad_local = jnp.dot(picked, weight_mat.T, preferred_element_type=jnp.float32).astype(jnp.bfloat16)
        start_col = (device * (col_count * TILE)).astype(jnp.int32)
        columns = lax.dynamic_slice_in_dim(hidden, start_col, col_count * TILE, 1)
        products = jnp.dot(columns.T, picked, preferred_element_type=jnp.float32)
        tile_grads = products.reshape(col_count, TILE, RSET, TILE).transpose(0, 2, 1, 3)
        tile_grads = tile_grads * mask_set[:, :, None, None].astype(jnp.float32)
        return grad_local, tile_grads

    grad_parts, tile_parts = lax.map(per_device, jnp.arange(N_SEQT, dtype=jnp.int32))
    grad_hidden = grad_parts.transpose(1, 0, 2).reshape(token_count, FF)
    grad_tiles = tile_parts.reshape(FF // TILE, RSET, TILE, TILE)
    return grad_hidden, grad_tiles
```

```python
import functools

import jax
import jax.numpy as jnp
from jax import lax
from jax.experimental import pallas as pl
from jax.experimental.pallas import tpu as pltpu
from jax.sharding import PartitionSpec as P

MESH = pl.DeviceIdType.MESH


def prepare(rb, mask, og, tiles, picked, weight):
    n, slots = rb.shape
    cols, _, tile, _ = tiles.shape
    for d in range(n):
        for k in range(slots):
            at = pl.multiple_of(rb[d, k] * tile, tile)
            picked[d, :, k * tile : (k + 1) * tile] = og[:, pl.ds(at, tile)]
    for c in range(cols):
        for k in range(slots):
            kept = tiles[c, k].astype(jnp.float32) * mask[c, k].astype(jnp.float32)
            weight[k * tile : (k + 1) * tile, c * tile : (c + 1) * tile] = kept.T.astype(weight.dtype)


def kernel(
    groups, n, nz, ny,
    mask, hid, picked, weight, gh, gt,
    rows, hbuf, wbuf,
    hsend, hrecv, rsend, rrecv, wrecv, zsend, ysend, xsend, csend, own_sem,
):
    g, me = lax.axis_index("groups"), lax.axis_index("seqt")
    core = me % 2
    chip = me // 2
    y, z = chip % ny, chip // ny
    tok = hid.shape[0]
    cols, slots, tile, _ = gt.shape
    width = cols * tile
    depth = slots * tile
    share = depth // groups

    def dev(zz, yy, cc):
        return (zz * ny + yy) * 2 + cc

    barrier = pltpu.get_barrier_semaphore()
    for i in range(1, n):
        pl.semaphore_signal(barrier, 1, device_id=(g, (me + i) % n), device_id_type=MESH)
    for i in range(1, groups):
        pl.semaphore_signal(barrier, 1, device_id=((g + i) % groups, me), device_id_type=MESH)

    own_hidden = pltpu.make_async_copy(
        hid.at[:, pl.ds(me * width, width)], hbuf.at[pl.ds(me * tok, tok), :], own_sem
    )
    own_hidden.start()
    wbuf[me] = weight[...]
    pl.semaphore_wait(barrier, n - 1 + groups - 1)

    def w_copy(d, part, sem, to):
        ref = wbuf.at[d, pl.ds(part * share, share), :]
        return pltpu.make_async_remote_copy(
            ref, ref, send_sem=sem, recv_sem=wrecv.at[d, part], device_id=to, device_id_type=MESH
        )

    def z_copy(way, zz):
        step = 1 if way == 0 else -1
        return w_copy(dev(zz, y, core), g, zsend.at[way, zz], (g, dev(z + step, y, core)))

    def y_copy(zz):
        return w_copy(dev(zz, y, core), g, ysend.at[zz], (g, dev(z, 1 - y, core)))

    def x_copy(zz, yy, i):
        return w_copy(dev(zz, yy, core), g, xsend.at[zz * ny + yy, i], ((g + i) % groups, me))

    def c_copy(zz, yy):
        d = dev(zz, yy, core)
        return pltpu.make_async_remote_copy(
            wbuf.at[d], wbuf.at[d], send_sem=csend.at[zz * ny + yy], recv_sem=wrecv.at[d, 0],
            device_id=(g, dev(z, y, 1 - core)), device_id_type=MESH,
        )

    def h_copy(i):
        p = (me + i) % n
        return pltpu.make_async_remote_copy(
            hid.at[:, pl.ds(p * width, width)], hbuf.at[pl.ds(me * tok, tok), :],
            send_sem=hsend.at[i], recv_sem=hrecv.at[me], device_id=(g, p), device_id_type=MESH,
        )

    def r_copy(i):
        p = (me + i) % n
        return pltpu.make_async_remote_copy(
            picked.at[p], rows.at[pl.ds(me * tok, tok), :],
            send_sem=rsend.at[i], recv_sem=rrecv.at[me], device_id=(g, p), device_id_type=MESH,
        )

    pl.when(z < nz - 1)(lambda: z_copy(0, z).start())
    pl.when(z > 0)(lambda: z_copy(1, z).start())
    if ny > 1:
        y_copy(z).start()
    c_copy(z, y).start()

    order = sorted(range(1, n), key=lambda i: abs(i - n // 2))
    for i in order:
        h_copy(i).start()
        r_copy(i).start()
    rows[pl.ds(me * tok, tok), :] = picked[me]
    gt[...] = jnp.zeros_like(gt)

    def to_groups(zz, yy):
        for i in range(1, groups):
            x_copy(zz, yy, i).start()

    def z_arrival(s, way):
        zz = z - s if way == 0 else z + s
        fits = (zz >= 0) if way == 0 else (zz < nz)
        more = (z < nz - 1) if way == 0 else (z > 0)

        @pl.when(fits)
        def _():
            w_copy(dev(zz, y, core), g, own_sem, (g, dev(z, y, 1 - core))).wait_recv()
            pl.when(more)(lambda: z_copy(way, zz).start())
            if ny > 1:
                y_copy(zz).start()
            to_groups(zz, y)

    def y_arrival(s, way):
        zz = z - s if way == 0 else z + s
        fits = (zz >= 0) if way == 0 else (zz < nz)

        @pl.when(fits)
        def _():
            w_copy(dev(zz, 1 - y, core), g, own_sem, (g, dev(z, y, 1 - core))).wait_recv()
            to_groups(zz, 1 - y)

    def x_arrival(s, way, yy):
        zz = z - s if way == 0 else z + s
        fits = (zz >= 0) if way == 0 else (zz < nz)

        @pl.when(fits)
        def _():
            for i in range(1, groups):
                w_copy(dev(zz, yy, core), (g + i) % groups, own_sem, (g, dev(z, y, 1 - core))).wait_recv()
            c_copy(zz, yy).start()

    def multiply(d):
        piece = min(width, 512)
        for c in range(width // piece):
            w = wbuf[d, :, c * piece : (c + 1) * piece]
            out = jnp.dot(picked[d], w, preferred_element_type=jnp.float32).astype(gh.dtype)
            gh[:, pl.ds(pl.multiple_of(d * width + c * piece, 128), piece)] = out

    def ways(s):
        return (0,) if s == 0 else (0, 1)

    for s in range(nz + 2):
        if 1 <= s < nz:
            for way in ways(s):
                z_arrival(s, way)
        if ny > 1 and 0 <= s - 1 < nz:
            for way in ways(s - 1):
                y_arrival(s - 1, way)
        if 0 <= s - 2 < nz:
            for way in ways(s - 2):
                if s - 2 > 0:
                    x_arrival(s - 2, way, y)
                if ny > 1:
                    x_arrival(s - 2, way, 1 - y)

    @pl.loop(0, n // 2)
    def _(j):
        multiply(j * 2 + core)

    own_hidden.wait()
    block = min(width, 256)

    @pl.loop(0, n // 2)
    def _(j):
        other = (chip + j) % (n // 2)
        for c in range(2):
            src = other * 2 + c

            @pl.when(src != me)
            def _():
                at = pl.ds(src * tok, tok)
                pltpu.make_async_remote_copy(
                    hbuf.at[at, :], hbuf.at[at, :], send_sem=own_sem, recv_sem=hrecv.at[src],
                    device_id=(g, dev(z, y, 1 - core)), device_id_type=MESH,
                ).wait_recv()
                pltpu.make_async_remote_copy(
                    rows.at[at, :], rows.at[at, :], send_sem=own_sem, recv_sem=rrecv.at[src],
                    device_id=(g, dev(z, y, 1 - core)), device_id_type=MESH,
                ).wait_recv()

        at = pl.ds(pl.multiple_of(other * 2 * tok, 2 * tok), 2 * tok)

        @pl.loop(0, width // block)
        def _(b):
            h = hbuf[at, pl.ds(pl.multiple_of(b * block, block), block)]
            prod = lax.dot_general(
                h, rows[at, :], (((0,), (0,)), ((), ())), preferred_element_type=jnp.float32
            )
            for c in range(block // tile):
                for k in range(slots):
                    part = prod[c * tile : (c + 1) * tile, k * tile : (k + 1) * tile]
                    gt[b * (block // tile) + c, k] += part

    for c in range(cols):
        for k in range(slots):
            gt[c, k] = gt[c, k] * mask[c, k].astype(jnp.float32)

    @pl.loop(0, n // 2)
    def _(j):
        d = j * 2 + 1 - core
        pltpu.make_async_remote_copy(
            wbuf.at[d], wbuf.at[d], send_sem=own_sem, recv_sem=wrecv.at[d, 0],
            device_id=(g, dev(z, y, 1 - core)), device_id_type=MESH,
        ).wait_recv()
        multiply(d)

    for i in range(1, n):
        h_copy(i).wait_send()
        r_copy(i).wait_send()
    for s in range(nz):
        for way in ways(s):
            for go in (0, 1) if s == 0 else (way,):
                zz = z - s if way == 0 else z + s
                fits = (zz >= 0) if way == 0 else (zz < nz)
                more = (z < nz - 1) if go == 0 else (z > 0)
                pl.when(fits & more)(functools.partial(lambda go, zz: z_copy(go, zz).wait_send(), go, zz))
    for zz in range(nz):
        if ny > 1:
            y_copy(zz).wait_send()
        for yy in range(ny):
            c_copy(zz, yy).wait_send()

            @pl.when((zz != z) | (yy != y))
            def _():
                for i in range(1, groups):
                    x_copy(zz, yy, i).wait_send()


def solution(mesh):
    groups, n = mesh.shape["groups"], mesh.shape["seqt"]
    nz = groups * n // 8
    ny = n // 2 // nz

    def on_device(out_grad, hidden, down_tiles, row_blocks, tile_mask):
        tok, ff = hidden.shape
        cols, slots, tile, _ = down_tiles.shape
        width, depth = cols * tile, slots * tile
        dma = pltpu.SemaphoreType.DMA
        vmem = pl.BlockSpec(memory_space=pltpu.VMEM)
        smem = pl.BlockSpec(memory_space=pltpu.SMEM)
        n_rows = row_blocks.shape[0]
        picked, weight = pl.pallas_call(
            prepare,
            out_shape=(
                jax.ShapeDtypeStruct((n_rows, tok, depth), jnp.bfloat16),
                jax.ShapeDtypeStruct((depth, width), jnp.bfloat16),
            ),
            in_specs=[smem, smem, vmem, vmem],
            out_specs=(vmem, vmem),
            compiler_params=pltpu.CompilerParams(vmem_limit_bytes=40 << 20),
        )(row_blocks, tile_mask, out_grad, down_tiles)
        return tuple(pl.pallas_call(
            functools.partial(kernel, groups, n, nz, ny),
            out_shape=(
                jax.ShapeDtypeStruct((tok, ff), jnp.bfloat16),
                jax.ShapeDtypeStruct((cols, slots, tile, tile), jnp.float32),
            ),
            in_specs=[smem, pl.BlockSpec(memory_space=pl.ANY), vmem, vmem],
            out_specs=(vmem, vmem),
            scratch_shapes=[
                pltpu.VMEM((n * tok, depth), jnp.bfloat16),
                pltpu.VMEM((n * tok, width), jnp.bfloat16),
                pltpu.VMEM((n, depth, width), jnp.bfloat16),
                dma((n,)), dma((n,)), dma((n,)), dma((n,)), dma((n, groups)),
                dma((2, nz)), dma((nz,)), dma((nz * ny, groups)), dma((nz * ny,)), dma(()),
            ],
            compiler_params=pltpu.CompilerParams(
                collective_id=0, has_side_effects=True, vmem_limit_bytes=56 << 20
            ),
            cost_estimate=pl.CostEstimate(
                flops=4 * n * tok * depth * width, bytes_accessed=20 << 20, transcendentals=0
            ),
        )(tile_mask, hidden, picked, weight))

    return jax.shard_map(
        on_device,
        mesh=mesh,
        in_specs=(
            P(("groups", "seqt"), None),
            P(("groups", "seqt"), None),
            P("seqt", None, None, None),
            P(),
            P("seqt", None),
        ),
        out_specs=(P(("groups", "seqt"), None), P(("groups", "seqt"), None, None, None)),
        check_vma=False,
    )
```

```python
import functools

import jax
import jax.numpy as jnp
from jax import lax
from jax.experimental import pallas as pl
from jax.experimental.pallas import tpu as pltpu
from jax.sharding import PartitionSpec as P

MESH = pl.DeviceIdType.MESH


def prepare(rb, mask, og, tiles, picked, weight):
    n, slots = rb.shape
    cols, _, tile, _ = tiles.shape
    for d in range(n):
        for k in range(slots):
            at = pl.multiple_of(rb[d, k] * tile, tile)
            picked[d, :, k * tile : (k + 1) * tile] = og[:, pl.ds(at, tile)]
    for c in range(cols):
        for k in range(slots):
            kept = tiles[c, k].astype(jnp.float32) * mask[c, k].astype(jnp.float32)
            weight[k * tile : (k + 1) * tile, c * tile : (c + 1) * tile] = kept.T.astype(weight.dtype)


FIRST, EACH = 3, 2


def send_order(n, nz):
    line = n // nz
    far = sorted(range(nz), key=lambda r: abs(2 * r - nz))
    return [0] + [i for q in range(line) for i in (line * r + q for r in far) if i]


def kernel(
    groups, n, nz, ny,
    mask, hid, picked, weight, gh, gt,
    rows, hbuf, wbuf,
    hsend, hrecv, rsend, rrecv, wrecv, zsend, ysend, xsend, csend, own_sem,
):
    g, me = lax.axis_index("groups"), lax.axis_index("seqt")
    core = me % 2
    chip = me // 2
    y, z = chip % ny, chip // ny
    tok = hid.shape[0]
    cols, slots, tile, _ = gt.shape
    width = cols * tile
    depth = slots * tile
    share = depth // groups

    def dev(zz, yy, cc):
        return (zz * ny + yy) * 2 + cc

    barrier = pltpu.get_barrier_semaphore()
    for i in range(1, n):
        pl.semaphore_signal(barrier, 1, device_id=(g, (me + i) % n), device_id_type=MESH)
    for i in range(1, groups):
        pl.semaphore_signal(barrier, 1, device_id=((g + i) % groups, me), device_id_type=MESH)

    order = send_order(n, nz)
    own_hidden = pltpu.make_async_copy(
        hid.at[:, pl.ds(me * width, width)], hbuf.at[pl.ds(0, tok), :], own_sem
    )
    own_hidden.start()
    wbuf[me] = weight[...]
    pl.semaphore_wait(barrier, n - 1 + groups - 1)

    def w_copy(d, part, sem, to):
        ref = wbuf.at[d, pl.ds(part * share, share), :]
        return pltpu.make_async_remote_copy(
            ref, ref, send_sem=sem, recv_sem=wrecv.at[d, part], device_id=to, device_id_type=MESH
        )

    def z_copy(way, zz):
        step = 1 if way == 0 else -1
        return w_copy(dev(zz, y, core), g, zsend.at[way, zz], (g, dev(z + step, y, core)))

    def y_copy(zz):
        return w_copy(dev(zz, y, core), g, ysend.at[zz], (g, dev(z, 1 - y, core)))

    def x_copy(zz, yy, i):
        return w_copy(dev(zz, yy, core), g, xsend.at[zz * ny + yy, i], ((g + i) % groups, me))

    def c_copy(zz, yy):
        d = dev(zz, yy, core)
        return pltpu.make_async_remote_copy(
            wbuf.at[d], wbuf.at[d], send_sem=csend.at[zz * ny + yy], recv_sem=wrecv.at[d, 0],
            device_id=(g, dev(z, y, 1 - core)), device_id_type=MESH,
        )

    def h_copy(q):
        p = (me + order[q]) % n
        return pltpu.make_async_remote_copy(
            hid.at[:, pl.ds(p * width, width)], hbuf.at[pl.ds(q * tok, tok), :],
            send_sem=hsend.at[q], recv_sem=hrecv.at[q], device_id=(g, p), device_id_type=MESH,
        )

    def r_copy(q):
        p = (me + order[q]) % n
        return pltpu.make_async_remote_copy(
            picked.at[p], rows.at[pl.ds(q * tok, tok), :],
            send_sem=rsend.at[q], recv_sem=rrecv.at[q], device_id=(g, p), device_id_type=MESH,
        )

    def send(first, last):
        for q in range(max(first, 1), min(last, n)):
            h_copy(q).start()
            r_copy(q).start()

    pl.when(z < nz - 1)(lambda: z_copy(0, z).start())
    pl.when(z > 0)(lambda: z_copy(1, z).start())
    if ny > 1:
        y_copy(z).start()
    c_copy(z, y).start()

    send(0, FIRST * n // 16)
    rows[pl.ds(0, tok), :] = picked[me]
    gt[...] = jnp.zeros_like(gt)

    def to_groups(zz, yy):
        for i in range(1, groups):
            x_copy(zz, yy, i).start()

    def z_arrival(s, way):
        zz = z - s if way == 0 else z + s
        fits = (zz >= 0) if way == 0 else (zz < nz)
        more = (z < nz - 1) if way == 0 else (z > 0)

        @pl.when(fits)
        def _():
            w_copy(dev(zz, y, core), g, own_sem, (g, dev(z, y, 1 - core))).wait_recv()
            pl.when(more)(lambda: z_copy(way, zz).start())
            if ny > 1:
                y_copy(zz).start()
            to_groups(zz, y)

    def y_arrival(s, way):
        zz = z - s if way == 0 else z + s
        fits = (zz >= 0) if way == 0 else (zz < nz)

        @pl.when(fits)
        def _():
            w_copy(dev(zz, 1 - y, core), g, own_sem, (g, dev(z, y, 1 - core))).wait_recv()
            to_groups(zz, 1 - y)

    def x_arrival(s, way, yy):
        zz = z - s if way == 0 else z + s
        fits = (zz >= 0) if way == 0 else (zz < nz)

        @pl.when(fits)
        def _():
            for i in range(1, groups):
                w_copy(dev(zz, yy, core), (g + i) % groups, own_sem, (g, dev(z, y, 1 - core))).wait_recv()
            c_copy(zz, yy).start()
            multiply(dev(zz, yy, core))

    def multiply(d):
        piece = min(width, 512)
        for c in range(width // piece):
            w = wbuf[d, :, c * piece : (c + 1) * piece]
            out = jnp.dot(picked[d], w, preferred_element_type=jnp.float32).astype(gh.dtype)
            gh[:, pl.ds(pl.multiple_of(d * width + c * piece, 128), piece)] = out

    def ways(s):
        return (0,) if s == 0 else (0, 1)

    def c_arrival(s, way, yy):
        zz = z - s if way == 0 else z + s
        fits = (zz >= 0) if way == 0 else (zz < nz)

        @pl.when(fits)
        def _():
            d = dev(zz, yy, 1 - core)
            pltpu.make_async_remote_copy(
                wbuf.at[d], wbuf.at[d], send_sem=own_sem, recv_sem=wrecv.at[d, 0],
                device_id=(g, dev(z, y, 1 - core)), device_id_type=MESH,
            ).wait_recv()
            multiply(d)

    block = min(width, 256)

    def accumulate(first):
        for q in (first, first + 1):
            if q == 0:
                own_hidden.wait()
            else:
                h_copy(q).wait_recv()
                r_copy(q).wait_recv()
        at = pl.ds(first * tok, 2 * tok)

        @pl.loop(0, width // block)
        def _(b):
            h = hbuf[at, pl.ds(pl.multiple_of(b * block, block), block)]
            prod = lax.dot_general(
                h, rows[at, :], (((0,), (0,)), ((), ())), preferred_element_type=jnp.float32
            )
            for c in range(block // tile):
                for k in range(slots):
                    part = prod[c * tile : (c + 1) * tile, k * tile : (k + 1) * tile]
                    gt[b * (block // tile) + c, k] += part

    done = 0
    for s in range(1, nz + 4):
        send((FIRST + (s - 1) * EACH) * n // 16, (FIRST + s * EACH) * n // 16 if s < nz + 3 else n)
        if s < nz:
            for way in ways(s):
                z_arrival(s, way)
        if ny > 1 and 0 <= s - 1 < nz:
            for way in ways(s - 1):
                y_arrival(s - 1, way)
        if 0 <= s - 2 < nz:
            for way in ways(s - 2):
                if s - 2 > 0:
                    x_arrival(s - 2, way, y)
                if ny > 1:
                    x_arrival(s - 2, way, 1 - y)
        if s == 1:
            multiply(me)
        ready = n if s == nz + 3 else max(0, (FIRST + (s - 2) * EACH) * n // 16)
        while done + 2 <= min(ready, n):
            accumulate(done)
            done += 2
        if 0 <= s - 3 < nz:
            for way in ways(s - 3):
                for yy in ((y, 1 - y) if ny > 1 else (y,)):
                    c_arrival(s - 3, way, yy)

    for c in range(cols):
        for k in range(slots):
            gt[c, k] = gt[c, k] * mask[c, k].astype(jnp.float32)

    for i in range(1, n):
        h_copy(i).wait_send()
        r_copy(i).wait_send()
    for s in range(nz):
        for way in ways(s):
            for go in (0, 1) if s == 0 else (way,):
                zz = z - s if way == 0 else z + s
                fits = (zz >= 0) if way == 0 else (zz < nz)
                more = (z < nz - 1) if go == 0 else (z > 0)
                pl.when(fits & more)(functools.partial(lambda go, zz: z_copy(go, zz).wait_send(), go, zz))
    for zz in range(nz):
        if ny > 1:
            y_copy(zz).wait_send()
        for yy in range(ny):
            c_copy(zz, yy).wait_send()

            @pl.when((zz != z) | (yy != y))
            def _():
                for i in range(1, groups):
                    x_copy(zz, yy, i).wait_send()


def solution(mesh):
    groups, n = mesh.shape["groups"], mesh.shape["seqt"]
    nz = groups * n // 8
    ny = n // 2 // nz

    def on_device(out_grad, hidden, down_tiles, row_blocks, tile_mask):
        tok, ff = hidden.shape
        cols, slots, tile, _ = down_tiles.shape
        width, depth = cols * tile, slots * tile
        dma = pltpu.SemaphoreType.DMA
        vmem = pl.BlockSpec(memory_space=pltpu.VMEM)
        smem = pl.BlockSpec(memory_space=pltpu.SMEM)
        n_rows = row_blocks.shape[0]
        picked, weight = pl.pallas_call(
            prepare,
            out_shape=(
                jax.ShapeDtypeStruct((n_rows, tok, depth), jnp.bfloat16),
                jax.ShapeDtypeStruct((depth, width), jnp.bfloat16),
            ),
            in_specs=[smem, smem, vmem, vmem],
            out_specs=(vmem, vmem),
            compiler_params=pltpu.CompilerParams(vmem_limit_bytes=40 << 20),
        )(row_blocks, tile_mask, out_grad, down_tiles)
        return tuple(pl.pallas_call(
            functools.partial(kernel, groups, n, nz, ny),
            out_shape=(
                jax.ShapeDtypeStruct((tok, ff), jnp.bfloat16),
                jax.ShapeDtypeStruct((cols, slots, tile, tile), jnp.float32),
            ),
            in_specs=[smem, pl.BlockSpec(memory_space=pl.ANY), vmem, vmem],
            out_specs=(vmem, vmem),
            scratch_shapes=[
                pltpu.VMEM((n * tok, depth), jnp.bfloat16),
                pltpu.VMEM((n * tok, width), jnp.bfloat16),
                pltpu.VMEM((n, depth, width), jnp.bfloat16),
                dma((n,)), dma((n,)), dma((n,)), dma((n,)), dma((n, groups)),
                dma((2, nz)), dma((nz,)), dma((nz * ny, groups)), dma((nz * ny,)), dma(()),
            ],
            compiler_params=pltpu.CompilerParams(
                collective_id=0, has_side_effects=True, vmem_limit_bytes=56 << 20
            ),
            cost_estimate=pl.CostEstimate(
                flops=4 * n * tok * depth * width, bytes_accessed=20 << 20, transcendentals=0
            ),
        )(tile_mask, hidden, picked, weight))

    return jax.shard_map(
        on_device,
        mesh=mesh,
        in_specs=(
            P(("groups", "seqt"), None),
            P(("groups", "seqt"), None),
            P("seqt", None, None, None),
            P(),
            P("seqt", None),
        ),
        out_specs=(P(("groups", "seqt"), None), P(("groups", "seqt"), None, None, None)),
        check_vma=False,
    )
```

```python
import functools

import jax
import jax.numpy as jnp
from jax import lax
from jax.experimental import pallas as pl
from jax.experimental.pallas import tpu as pltpu
from jax.sharding import PartitionSpec as P

MESH = pl.DeviceIdType.MESH


def prepare(rb, mask, og, tiles, picked, weight):
    n, slots = rb.shape
    cols, _, tile, _ = tiles.shape
    for d in range(n):
        for k in range(slots):
            at = pl.multiple_of(rb[d, k] * tile, tile)
            picked[d, :, k * tile : (k + 1) * tile] = og[:, pl.ds(at, tile)]
    for c in range(cols):
        for k in range(slots):
            kept = tiles[c, k].astype(jnp.float32) * mask[c, k].astype(jnp.float32)
            weight[k * tile : (k + 1) * tile, c * tile : (c + 1) * tile] = kept.T.astype(weight.dtype)


FIRST, EACH = 2, 3


def send_order(n, nz):
    line = n // nz
    far = sorted(range(nz), key=lambda r: abs(2 * r - nz))
    return [0] + [i for q in range(line) for i in (line * r + q for r in far) if i]


def kernel(
    groups, n, nz, ny,
    mask, hid, picked, weight, gh, gt,
    rows, hbuf, wbuf,
    hsend, hrecv, rsend, rrecv, wrecv, zsend, ysend, xsend, csend, own_sem,
):
    g, me = lax.axis_index("groups"), lax.axis_index("seqt")
    core = me % 2
    chip = me // 2
    y, z = chip % ny, chip // ny
    tok = hid.shape[0]
    cols, slots, tile, _ = gt.shape
    width = cols * tile
    depth = slots * tile
    share = depth // groups

    def dev(zz, yy, cc):
        return (zz * ny + yy) * 2 + cc

    barrier = pltpu.get_barrier_semaphore()
    for i in range(1, n):
        pl.semaphore_signal(barrier, 1, device_id=(g, (me + i) % n), device_id_type=MESH)
    for i in range(1, groups):
        pl.semaphore_signal(barrier, 1, device_id=((g + i) % groups, me), device_id_type=MESH)

    order = send_order(n, nz)
    own_hidden = pltpu.make_async_copy(
        hid.at[:, pl.ds(me * width, width)], hbuf.at[pl.ds(0, tok), :], own_sem
    )
    own_hidden.start()
    wbuf[me] = weight[...]
    pl.semaphore_wait(barrier, n - 1 + groups - 1)

    def w_copy(d, part, sem, to):
        ref = wbuf.at[d, pl.ds(part * share, share), :]
        return pltpu.make_async_remote_copy(
            ref, ref, send_sem=sem, recv_sem=wrecv.at[d, part], device_id=to, device_id_type=MESH
        )

    def z_copy(way, zz):
        step = 1 if way == 0 else -1
        return w_copy(dev(zz, y, core), g, zsend.at[way, zz], (g, dev(z + step, y, core)))

    def y_copy(zz):
        return w_copy(dev(zz, y, core), g, ysend.at[zz], (g, dev(z, 1 - y, core)))

    def x_copy(zz, yy, i):
        return w_copy(dev(zz, yy, core), g, xsend.at[zz * ny + yy, i], ((g + i) % groups, me))

    def c_copy(zz, yy):
        d = dev(zz, yy, core)
        return pltpu.make_async_remote_copy(
            wbuf.at[d], wbuf.at[d], send_sem=csend.at[zz * ny + yy], recv_sem=wrecv.at[d, 0],
            device_id=(g, dev(z, y, 1 - core)), device_id_type=MESH,
        )

    def h_copy(q):
        p = (me + order[q]) % n
        return pltpu.make_async_remote_copy(
            hid.at[:, pl.ds(p * width, width)], hbuf.at[pl.ds(q * tok, tok), :],
            send_sem=hsend.at[q], recv_sem=hrecv.at[q], device_id=(g, p), device_id_type=MESH,
        )

    def r_copy(q):
        p = (me + order[q]) % n
        return pltpu.make_async_remote_copy(
            picked.at[p], rows.at[pl.ds(q * tok, tok), :],
            send_sem=rsend.at[q], recv_sem=rrecv.at[q], device_id=(g, p), device_id_type=MESH,
        )

    def send(first, last):
        for q in range(max(first, 1), min(last, n)):
            h_copy(q).start()
            r_copy(q).start()

    pl.when(z < nz - 1)(lambda: z_copy(0, z).start())
    pl.when(z > 0)(lambda: z_copy(1, z).start())
    if ny > 1:
        y_copy(z).start()
    c_copy(z, y).start()

    send(0, FIRST * n // 16)
    rows[pl.ds(0, tok), :] = picked[me]
    gt[...] = jnp.zeros_like(gt)

    def to_groups(zz, yy):
        for i in range(1, groups):
            x_copy(zz, yy, i).start()

    def z_arrival(s, way):
        zz = z - s if way == 0 else z + s
        fits = (zz >= 0) if way == 0 else (zz < nz)
        more = (z < nz - 1) if way == 0 else (z > 0)

        @pl.when(fits)
        def _():
            w_copy(dev(zz, y, core), g, own_sem, (g, dev(z, y, 1 - core))).wait_recv()
            pl.when(more)(lambda: z_copy(way, zz).start())
            if ny > 1:
                y_copy(zz).start()
            to_groups(zz, y)

    def y_arrival(s, way):
        zz = z - s if way == 0 else z + s
        fits = (zz >= 0) if way == 0 else (zz < nz)

        @pl.when(fits)
        def _():
            w_copy(dev(zz, 1 - y, core), g, own_sem, (g, dev(z, y, 1 - core))).wait_recv()
            to_groups(zz, 1 - y)

    def x_arrival(s, way, yy):
        zz = z - s if way == 0 else z + s
        fits = (zz >= 0) if way == 0 else (zz < nz)

        @pl.when(fits)
        def _():
            for i in range(1, groups):
                w_copy(dev(zz, yy, core), (g + i) % groups, own_sem, (g, dev(z, y, 1 - core))).wait_recv()
            c_copy(zz, yy).start()
            multiply(dev(zz, yy, core))

    def multiply(d):
        piece = min(width, 512)
        for c in range(width // piece):
            w = wbuf[d, :, c * piece : (c + 1) * piece]
            out = jnp.dot(picked[d], w, preferred_element_type=jnp.float32).astype(gh.dtype)
            gh[:, pl.ds(pl.multiple_of(d * width + c * piece, 128), piece)] = out

    def ways(s):
        return (0,) if s == 0 else (0, 1)

    def c_arrival(s, way, yy):
        zz = z - s if way == 0 else z + s
        fits = (zz >= 0) if way == 0 else (zz < nz)

        @pl.when(fits)
        def _():
            d = dev(zz, yy, 1 - core)
            pltpu.make_async_remote_copy(
                wbuf.at[d], wbuf.at[d], send_sem=own_sem, recv_sem=wrecv.at[d, 0],
                device_id=(g, dev(z, y, 1 - core)), device_id_type=MESH,
            ).wait_recv()
            multiply(d)

    block = min(width, 256)

    def accumulate(first):
        for q in (first, first + 1):
            if q == 0:
                own_hidden.wait()
            else:
                h_copy(q).wait_recv()
                r_copy(q).wait_recv()
        at = pl.ds(first * tok, 2 * tok)

        @pl.loop(0, width // block)
        def _(b):
            h = hbuf[at, pl.ds(pl.multiple_of(b * block, block), block)]
            prod = lax.dot_general(
                h, rows[at, :], (((0,), (0,)), ((), ())), preferred_element_type=jnp.float32
            )
            for c in range(block // tile):
                for k in range(slots):
                    part = prod[c * tile : (c + 1) * tile, k * tile : (k + 1) * tile]
                    gt[b * (block // tile) + c, k] += part

    done = 0
    for s in range(1, nz + 4):
        send((FIRST + (s - 1) * EACH) * n // 16, (FIRST + s * EACH) * n // 16 if s < nz + 3 else n)
        if s < nz:
            for way in ways(s):
                z_arrival(s, way)
        if ny > 1 and 0 <= s - 1 < nz:
            for way in ways(s - 1):
                y_arrival(s - 1, way)
        if 0 <= s - 2 < nz:
            for way in ways(s - 2):
                if s - 2 > 0:
                    x_arrival(s - 2, way, y)
                if ny > 1:
                    x_arrival(s - 2, way, 1 - y)
        if s == 1:
            multiply(me)
        ready = n if s == nz + 3 else max(0, (FIRST + (s - 2) * EACH) * n // 16)
        while done + 2 <= min(ready, n):
            accumulate(done)
            done += 2
        if 0 <= s - 3 < nz:
            for way in ways(s - 3):
                for yy in ((y, 1 - y) if ny > 1 else (y,)):
                    c_arrival(s - 3, way, yy)

    for c in range(cols):
        for k in range(slots):
            gt[c, k] = gt[c, k] * mask[c, k].astype(jnp.float32)

    for i in range(1, n):
        h_copy(i).wait_send()
        r_copy(i).wait_send()
    for s in range(nz):
        for way in ways(s):
            for go in (0, 1) if s == 0 else (way,):
                zz = z - s if way == 0 else z + s
                fits = (zz >= 0) if way == 0 else (zz < nz)
                more = (z < nz - 1) if go == 0 else (z > 0)
                pl.when(fits & more)(functools.partial(lambda go, zz: z_copy(go, zz).wait_send(), go, zz))
    for zz in range(nz):
        if ny > 1:
            y_copy(zz).wait_send()
        for yy in range(ny):
            c_copy(zz, yy).wait_send()

            @pl.when((zz != z) | (yy != y))
            def _():
                for i in range(1, groups):
                    x_copy(zz, yy, i).wait_send()


def solution(mesh):
    groups, n = mesh.shape["groups"], mesh.shape["seqt"]
    nz = groups * n // 8
    ny = n // 2 // nz

    def on_device(out_grad, hidden, down_tiles, row_blocks, tile_mask):
        tok, ff = hidden.shape
        cols, slots, tile, _ = down_tiles.shape
        width, depth = cols * tile, slots * tile
        dma = pltpu.SemaphoreType.DMA
        vmem = pl.BlockSpec(memory_space=pltpu.VMEM)
        smem = pl.BlockSpec(memory_space=pltpu.SMEM)
        n_rows = row_blocks.shape[0]
        picked, weight = pl.pallas_call(
            prepare,
            out_shape=(
                jax.ShapeDtypeStruct((n_rows, tok, depth), jnp.bfloat16),
                jax.ShapeDtypeStruct((depth, width), jnp.bfloat16),
            ),
            in_specs=[smem, smem, vmem, vmem],
            out_specs=(vmem, vmem),
            compiler_params=pltpu.CompilerParams(vmem_limit_bytes=40 << 20),
        )(row_blocks, tile_mask, out_grad, down_tiles)
        return tuple(pl.pallas_call(
            functools.partial(kernel, groups, n, nz, ny),
            out_shape=(
                jax.ShapeDtypeStruct((tok, ff), jnp.bfloat16),
                jax.ShapeDtypeStruct((cols, slots, tile, tile), jnp.float32),
            ),
            in_specs=[smem, pl.BlockSpec(memory_space=pl.ANY), vmem, vmem],
            out_specs=(vmem, vmem),
            scratch_shapes=[
                pltpu.VMEM((n * tok, depth), jnp.bfloat16),
                pltpu.VMEM((n * tok, width), jnp.bfloat16),
                pltpu.VMEM((n, depth, width), jnp.bfloat16),
                dma((n,)), dma((n,)), dma((n,)), dma((n,)), dma((n, groups)),
                dma((2, nz)), dma((nz,)), dma((nz * ny, groups)), dma((nz * ny,)), dma(()),
            ],
            compiler_params=pltpu.CompilerParams(
                collective_id=0, has_side_effects=True, vmem_limit_bytes=56 << 20
            ),
            cost_estimate=pl.CostEstimate(
                flops=4 * n * tok * depth * width, bytes_accessed=20 << 20, transcendentals=0
            ),
        )(tile_mask, hidden, picked, weight))

    return jax.shard_map(
        on_device,
        mesh=mesh,
        in_specs=(
            P(("groups", "seqt"), None),
            P(("groups", "seqt"), None),
            P("seqt", None, None, None),
            P(),
            P("seqt", None),
        ),
        out_specs=(P(("groups", "seqt"), None), P(("groups", "seqt"), None, None, None)),
        check_vma=False,
    )
```
